32 devices in a mesh: groups: 2 (over x), wide: 16 (over z, y, core).
Axes of the slice: x: 2, y: 2, z: 4, core: 2. Of those that a mesh axis runs over, the one named last changes fastest.
Arguments:
- tokens: bfloat16 [768, 8192], P(('groups', 'wide')), parts along dimension 0, may hold values from -6 to 6
- gate_weight: bfloat16 [8192, 14336], P(None, 'wide'), may hold values from -0.0625 to 0.0625
- up_weight: bfloat16 [8192, 14336], P(None, 'wide'), may hold values from -0.0625 to 0.0625
- adapter_in: bfloat16 [32, 64, 8192], P(('groups', 'wide')), parts along dimension 0, may hold values from -0.0625 to 0.0625
- adapter_out: bfloat16 [32, 64, 14336], P('groups', None, 'wide'), parts along dimension 0, may hold values from -0.75 to 0.75
- seg_adapter: int32 [6], P('groups'), parts along dimension 0, may hold values from 0 to 15
- holder_slot: int32 [32], P('groups'), parts along dimension 0, may hold values from 0 to 15, each once
- seg_length: int32 [6], P('groups'), parts along dimension 0, may hold values from 1 to 128, 288 in all
Outputs:
- hidden: bfloat16 [768, 14336], P('groups', 'wide'), parts along dimension 0
The draws below stay inside these ranges and needn't reach their ends.
There are 2 independent parts, one for each index of `groups`. The reference program is written for one: setup_inputs(seed, part) draws one part's arguments, and reference() takes and returns one part's arrays. A program takes and returns all parts, laid end to end along the dimension named above; an argument that names none is the same for every part. Nothing has to cross between parts.
Inputs may be any that keep to these rules, and one draw needn't show every extreme that they name: `seg_adapter`: an adapter id below 16; several segments may name the same adapter. `holder_slot`: each slot once; the input map of slot k lives on device k // 1 of wide, as that device's local adapter k % 1. `seg_length`: the live rows stand first in their segment.
All inputs are finite; a program needn't handle non-finite values.
Results may differ from the reference program's by a relative error of at most 0.0035.
Values may be sent and summed in bfloat16 or wider, within the bound.
A program may use at most 128 MiB of HBM per device.

```python
import math
import jax
import jax.numpy as jnp
import numpy as np
from jax import lax

D = 8192
HIDDEN_WIDTH = 14336
R = 64
SEG = 128
TOTAL_ROWS = 384
SEGS = 3
ADAPTERS = 16


def steps_of(own_key, extent, pieces, smallest, high):
    def one(axis_at, shards_of):
        heights = jax.random.uniform(jax.random.fold_in(jax.random.fold_in(own_key, 6), axis_at), (shards_of,), jnp.float32, smallest / len(pieces), high / len(pieces))
        return jnp.repeat(jnp.exp(heights), extent[axis_at] // shards_of).reshape((-1,) + (1,) * (len(extent) - axis_at - 1))

    level = one(*pieces[0])
    for cut in pieces[1:]:
        level = level * one(*cut)
    return level


def cumulative_ranks(amount, slope):
    portions = [(1 << 20) // math.isqrt(grade ** slope) + 1 for grade in range(1, amount + 1)]
    deviation = 1 + sum(portions) // (1 << 30)
    return np.cumsum(np.array([max(1, weight // deviation) for weight in portions]))


def ranked_ids(rng, shape, number_of, lean):
    listing = cumulative_ranks(number_of, lean)
    pick = jax.random.randint(jax.random.fold_in(rng, 1), shape, 0, int(listing[number_of - 1]))
    grade = jnp.searchsorted(jnp.asarray(listing, jnp.int32), pick, side="right")
    return jax.random.permutation(jax.random.fold_in(rng, 2), number_of)[grade].astype(jnp.int32)


def length_profile(number_of, total, reach, skew):
    loads = [(1 << 20) // math.isqrt(grade ** skew) + 1 for grade in range(2, number_of + 1)]
    spare, given = total - reach - (number_of - 1), [1] * (number_of - 1)
    while spare > 0:
        movable = [i for i in range(number_of - 1) if given[i] < reach]
        whole, remaining = sum([loads[i] for i in movable]), spare
        for i in movable:
            more = min(reach - given[i], max(1, remaining * loads[i] // whole), spare)
            given[i] = given[i] + more
            spare = spare - more
    return np.array([reach] + given)


def ragged(stream_key, count, total, reach, slope):
    if count == 2:
        one = jax.random.randint(stream_key, (), max(1, total - reach), min(reach, total - 1) + 1)
        return jnp.stack([one, total - one])
    lengths = jnp.asarray(length_profile(count, total, reach, slope), jnp.int32)
    pairs = (count - 1) // 2
    source_of, receiver = lengths[1:1 + 2 * pairs:2], lengths[2:2 + 2 * pairs:2]
    slack = jnp.minimum(source_of - 1, reach - receiver)
    moved = jax.random.randint(jax.random.fold_in(stream_key, 1), (pairs,), 0, 1 << 20) % (slack + 1)
    lengths = lengths.at[1:1 + 2 * pairs:2].set(source_of - moved).at[2:2 + 2 * pairs:2].set(receiver + moved)
    return lengths[jax.random.permutation(jax.random.fold_in(stream_key, 2), count)]


def centred(rng, dims, width, most, split=(), kind=jnp.bfloat16):
    gain = steps_of(rng, dims, split, -0.22, 0.18) if split else 1.0
    entries = jax.random.normal(rng, dims, jnp.float32) * width * gain
    return jnp.minimum(jnp.maximum(entries, -most), most).astype(kind)


def setup_inputs(seed: int = 0, part: int = 0) -> dict:
    arg_keys = jax.random.split(jax.random.key(seed), 9)
    part_splits = jax.random.split(jax.random.fold_in(arg_keys[8], part), 9)
    tokens = centred(part_splits[0], (TOTAL_ROWS, D), 1.0, 6.0, ((0, 16),))
    gate_weight = centred(arg_keys[1], (D, HIDDEN_WIDTH), D ** -0.5, 0.0625, ((1, 16),))
    up_weight = centred(arg_keys[2], (D, HIDDEN_WIDTH), D ** -0.5, 0.0625, ((1, 16),))
    adapter_in = centred(part_splits[3], (ADAPTERS, R, D), D ** -0.5, 0.0625, ((0, 16),))
    adapter_out = centred(part_splits[4], (ADAPTERS, R, HIDDEN_WIDTH), R ** -0.5, 0.75, ((2, 16),))
    seg_adapter = ranked_ids(part_splits[5], (SEGS,), ADAPTERS, 2)
    holder_slot = jax.random.permutation(part_splits[6], ADAPTERS).astype(jnp.int32)
    seg_length = ragged(part_splits[7], SEGS, SEGS * SEG * 3 // 4, SEG, 0).astype(jnp.int32)
    return dict(tokens=tokens, gate_weight=gate_weight, up_weight=up_weight, adapter_in=adapter_in, adapter_out=adapter_out, seg_adapter=seg_adapter, holder_slot=holder_slot, seg_length=seg_length)


adapter_scale = 0.5


def reference(tokens, gate_weight, up_weight, adapter_in, adapter_out, seg_adapter, holder_slot, seg_length):
    gate_part = jnp.dot(tokens, gate_weight, preferred_element_type=jnp.float32)
    base_up_output = jnp.dot(tokens, up_weight, preferred_element_type=jnp.float32)
    seg_slot = holder_slot[seg_adapter].astype(jnp.int32)
    seg_rows = tokens.reshape(SEGS, SEG, D).astype(jnp.float32)
    chosen_in = adapter_in[seg_slot].astype(jnp.float32)
    reduced_rank_state = jnp.einsum("sqd,srd->sqr", seg_rows, chosen_in).astype(jnp.bfloat16)
    reduced_rank_state = lax.optimization_barrier(reduced_rank_state).astype(jnp.float32)
    selected_output = adapter_out[seg_slot].astype(jnp.float32)
    adapter_term = jnp.einsum("iyg,ign->iyn", reduced_rank_state, selected_output).reshape(TOTAL_ROWS, HIDDEN_WIDTH)
    up_output_total = base_up_output + adapter_scale * adapter_term
    positions = jnp.arange(SEG, dtype=jnp.int32)
    live_rows = (positions[None, :] < seg_length[:, None]).reshape(TOTAL_ROWS)
    hidden = jnp.where(live_rows[:, None], jax.nn.silu(gate_part) * up_output_total, jnp.float32(0.0))
    return hidden.astype(jnp.bfloat16)
```

```python
import functools

import jax
import jax.numpy as jnp
from jax import lax
from jax.experimental import pallas as pl
from jax.experimental.pallas import tpu as pltpu
from jax.sharding import PartitionSpec as P

adapter_scale = 0.5
MESH = pl.DeviceIdType.MESH
WINDOWS = 4
PARTS = 2


def kernel(
    n, seg_count,
    seg_adapter, holder_slot, seg_length, tokens, gate_weight, up_weight, adapter_in, adapter_out,
    hidden,
    gathered, weights, inmap, outmap, acc, low_acc, swap_out, swap_in, low_parts, low_sum,
    weight_sem, map_sem, swap_sem, ring_send, ring_recv, pair_send, pair_recv,
    low_send, low_recv, all_send, all_recv,
):
    me = lax.axis_index("wide")
    chips = n // 2
    depth = chips // 2
    steps = chips - 1
    chip, core = me // 2, me % 2
    zi, yi = chip // 2, chip % 2
    pos = zi + yi * (2 * depth - 1 - 2 * zi)
    pair = chip * 2 + 1 - core
    rows, columns = hidden.shape
    chip_rows = rows // chips
    own_rows = rows // n
    half_dim = tokens.shape[1] // 2
    width = gathered.shape[-1]
    part = width // PARTS
    seg_size = rows // seg_count

    def chip_at(q):
        side = q // depth
        return (q + side * (2 * depth - 1 - 2 * q)) * 2 + side

    def block_of(half, way, win):
        return (half * 2 + way) * WINDOWS + win

    def weight_copy(mat, half, way, win):
        block = block_of(half, way, win)
        source = (gate_weight, up_weight)[mat]
        return pltpu.make_async_copy(
            source.at[pl.ds(pl.multiple_of(block * width, width), width), :],
            weights.at[mat, block],
            weight_sem.at[mat, block],
        )

    inmap_copy = pltpu.make_async_copy(adapter_in.at[0], inmap, map_sem.at[0])
    outmap_copy = pltpu.make_async_copy(adapter_out, outmap, map_sem.at[1])

    barrier = pltpu.get_barrier_semaphore()
    for i in range(1, n):
        pl.semaphore_signal(
            barrier, inc=1, device_id={"wide": lax.rem(me + i, n)}, device_id_type=MESH
        )
    other = tokens[:, pl.ds(pl.multiple_of((1 - core) * half_dim, half_dim), half_dim)]
    pad = jnp.zeros((swap_out.shape[0] - own_rows, half_dim), jnp.float32)
    swap_out[...] = jnp.concatenate([other.astype(jnp.float32), pad], axis=0).astype(jnp.bfloat16)
    pl.semaphore_wait(barrier, n - 1)

    swap = pltpu.make_async_remote_copy(
        src_ref=swap_out, dst_ref=swap_in, send_sem=swap_sem.at[0], recv_sem=swap_sem.at[1],
        device_id={"wide": pair}, device_id_type=MESH,
    )
    swap.start()
    inmap_copy.start()
    for win in range(WINDOWS):
        for half in range(2):
            for way in range(2):
                for mat in range(2):
                    weight_copy(mat, half, way, win).start()
    outmap_copy.start()
    swap.wait()

    def rows_of(origin):
        return pl.ds(pl.multiple_of(chip_at(origin) * chip_rows, 16), chip_rows)

    def ring_copy(way, win, cut, step, origin):
        sign = 1 - 2 * way
        target = chip_at((pos + sign + chips) % chips) * 2 + core
        place = gathered.at[core, way, win, rows_of(origin), pl.ds(cut * part, part)]
        return pltpu.make_async_remote_copy(
            src_ref=place, dst_ref=place,
            send_sem=ring_send.at[way, win, cut, step], recv_sem=ring_recv.at[way, win, cut, step],
            device_id={"wide": target}, device_id_type=MESH,
        )

    def pair_copy(half, way, win, step, origin):
        place = gathered.at[half, way, win, rows_of(origin), :]
        return pltpu.make_async_remote_copy(
            src_ref=place, dst_ref=place,
            send_sem=pair_send.at[way, win, step], recv_sem=pair_recv.at[way, win, step],
            device_id={"wide": pair}, device_id_type=MESH,
        )

    def origin_at(way, step):
        sign = 1 - 2 * way
        return (pos - sign * step + 2 * chips) % chips

    def send_own(win):
        for cut in range(PARTS):
            for way in range(2):
                ring_copy(way, win, cut, 0, pos).start()
        for way in range(2):
            pair_copy(core, way, win, 0, pos).start()

    for win in range(WINDOWS):
        for way in range(2):
            at = (way * WINDOWS + win) * width
            mine = tokens[:, pl.ds(pl.multiple_of(core * half_dim + at, width), width)]
            mine = mine.astype(jnp.float32)
            theirs = swap_in[:, at:at + width].astype(jnp.float32)[:own_rows]
            first = jnp.where(core == 0, mine, theirs)
            second = jnp.where(core == 0, theirs, mine)
            gathered[core, way, win, rows_of(pos), :] = jnp.concatenate(
                [first, second], axis=0
            ).astype(jnp.bfloat16)
        if win == 0:
            send_own(0)

    acc[...] = jnp.zeros_like(acc)
    low_acc[...] = jnp.zeros_like(low_acc)
    inmap_copy.wait()

    def wait_pair(way, win):
        def one(step, carry):
            pair_copy(1 - core, way, win, step, origin_at(way, step)).wait_recv()
            return carry
        lax.fori_loop(0, chips, one, 0)

    def low_piece(win, half, way):
        at = pl.multiple_of(block_of(half, way, win) * width, width)
        low_acc[...] += lax.dot_general(
            gathered[half, way, win], inmap[:, pl.ds(at, width)],
            (((1,), (1,)), ((), ())), preferred_element_type=jnp.float32,
        )

    def main_piece(win, index, with_low):
        mat, way, half = index % 2, (index // 2) % 2, (core + index // 4) % 2
        block = block_of(half, way, win)
        if with_low:
            @pl.when((mat == 0) & (index >= 4))
            def _():
                wait_pair(way, win)

            @pl.when(mat == 0)
            def _():
                low_piece(win, half, way)
        pltpu.make_async_copy(
            gate_weight.at[pl.ds(0, width), :], weights.at[mat, block], weight_sem.at[mat, block]
        ).wait()
        acc[mat] += jnp.dot(
            gathered[half, way, win], weights[mat, block], preferred_element_type=jnp.float32
        )

    def round_of(t, carry):
        win, step = t // steps, t % steps
        for cut in range(PARTS):
            for way in range(2):
                origin = origin_at(way, step + 1)
                ring_copy(way, win, cut, step, origin).wait_recv()

                @pl.when(step < steps - 1)
                def _():
                    ring_copy(way, win, cut, step + 1, origin).start()
        for way in range(2):
            pair_copy(core, way, win, step + 1, origin_at(way, step + 1)).start()

        @pl.when((step == steps - 2) & (win < WINDOWS - 1))
        def _():
            send_own(win + 1)

        @pl.when(win > 0)
        def _():
            first = (step * 8) // steps
            count = ((step + 1) * 8) // steps - first

            def piece(i, c):
                main_piece(win - 1, first + i, True)
                return c
            lax.fori_loop(0, count, piece, 0)
        return carry

    lax.fori_loop(0, WINDOWS * steps, round_of, 0)

    last = WINDOWS - 1
    for way in range(2):
        low_piece(last, core, way)
    for way in range(2):
        wait_pair(way, last)
        low_piece(last, 1 - core, way)

    slots = [holder_slot[seg_adapter[s]] for s in range(seg_count)]
    kept = jnp.concatenate(
        [
            jnp.where(slots[s] == me, low_acc[s * seg_size:(s + 1) * seg_size, :], 0.0)
            for s in range(seg_count)
        ],
        axis=0,
    )
    low_acc[...] = kept

    def own_slice(device):
        return pl.ds(pl.multiple_of(device * own_rows, 8), own_rows)

    def low_copy(i):
        target = lax.rem(me + i, n)
        return pltpu.make_async_remote_copy(
            src_ref=low_acc.at[own_slice(target), :], dst_ref=low_parts.at[i],
            send_sem=low_send.at[i], recv_sem=low_recv.at[i],
            device_id={"wide": target}, device_id_type=MESH,
        )

    def all_copy(i):
        target = lax.rem(me + i, n)
        place = low_sum.at[own_slice(me), :]
        return pltpu.make_async_remote_copy(
            src_ref=place, dst_ref=place, send_sem=all_send.at[i], recv_sem=all_recv.at[i],
            device_id={"wide": target}, device_id_type=MESH,
        )

    def all_arrived(i):
        place = low_sum.at[own_slice(lax.rem(me + n - i, n)), :]
        return pltpu.make_async_remote_copy(
            src_ref=place, dst_ref=place, send_sem=all_send.at[i], recv_sem=all_recv.at[i],
            device_id={"wide": lax.rem(me + i, n)}, device_id_type=MESH,
        )

    for i in range(1, n):
        low_copy(i).start()

    def early(i, c):
        main_piece(last, i, False)
        return c

    lax.fori_loop(0, 4, early, 0)
    for i in range(1, n):
        low_copy(i).wait_recv()
    total = low_acc[own_slice(me), :]
    for i in range(1, n):
        total = total + low_parts[i]
    low_sum[own_slice(me), :] = total
    for i in range(1, n):
        all_copy(i).start()
    lax.fori_loop(4, 8, early, 0)
    acc[0] = acc[0] / (1.0 + jnp.exp(-acc[0]))
    outmap_copy.wait()
    for i in range(1, n):
        all_arrived(i).wait_recv()
    for s in range(seg_count):
        at = s * seg_size
        low = low_sum[at:at + seg_size, :].astype(jnp.bfloat16)
        term = jnp.dot(low, outmap[slots[s]], preferred_element_type=jnp.float32)
        value = acc[0, at:at + seg_size, :] * (
            acc[1, at:at + seg_size, :] + adapter_scale * term
        )
        position = lax.broadcasted_iota(jnp.int32, value.shape, 0)
        hidden[at:at + seg_size, :] = jnp.where(
            position < seg_length[s], value, 0.0
        ).astype(hidden.dtype)

    for i in range(1, n):
        low_copy(i).wait_send()
        all_copy(i).wait_send()

    def drain(t, carry):
        win, step = t // steps, t % steps
        for way in range(2):
            for cut in range(PARTS):
                ring_copy(way, win, cut, step, pos).wait_send()
            pair_copy(core, way, win, step, pos).wait_send()

            @pl.when(step == 0)
            def _():
                pair_copy(core, way, win, steps, pos).wait_send()
        return carry

    lax.fori_loop(0, WINDOWS * steps, drain, 0)


def fused(
    tokens, gate_weight, up_weight, adapter_in, adapter_out, seg_adapter, holder_slot, seg_length
):
    n = lax.axis_size("wide")
    rows = tokens.shape[0] * n
    dim = tokens.shape[1]
    columns = gate_weight.shape[1]
    rank = adapter_in.shape[1]
    chips = n // 2
    width = dim // 4 // WINDOWS
    dma = pltpu.SemaphoreType.DMA
    smem = pl.BlockSpec(memory_space=pltpu.SMEM)
    hbm = pl.BlockSpec(memory_space=pl.ANY)
    vmem = pl.BlockSpec(memory_space=pltpu.VMEM)
    return pl.pallas_call(
        functools.partial(kernel, n, seg_adapter.shape[0]),
        out_shape=jax.ShapeDtypeStruct((rows, columns), jnp.bfloat16),
        in_specs=[smem, smem, smem, vmem, hbm, hbm, hbm, hbm],
        out_specs=vmem,
        scratch_shapes=[
            pltpu.VMEM((2, 2, WINDOWS, rows, width), jnp.bfloat16),
            pltpu.VMEM((2, 4 * WINDOWS, width, columns), jnp.bfloat16),
            pltpu.VMEM((rank, dim), jnp.bfloat16),
            pltpu.VMEM(adapter_out.shape, jnp.bfloat16),
            pltpu.VMEM((2, rows, columns), jnp.float32),
            pltpu.VMEM((rows, rank), jnp.float32),
            pltpu.VMEM((32, dim // 2), jnp.bfloat16),
            pltpu.VMEM((32, dim // 2), jnp.bfloat16),
            pltpu.VMEM((n, rows // n, rank), jnp.float32),
            pltpu.VMEM((rows, rank), jnp.float32),
            dma((2, 4 * WINDOWS)),
            dma((2,)),
            dma((2,)),
            dma((2, WINDOWS, PARTS, chips - 1)),
            dma((2, WINDOWS, PARTS, chips - 1)),
            dma((2, WINDOWS, chips)),
            dma((2, WINDOWS, chips)),
            dma((n,)),
            dma((n,)),
            dma((n,)),
            dma((n,)),
        ],
        compiler_params=pltpu.CompilerParams(
            collective_id=0, has_side_effects=True, vmem_limit_bytes=60 * 1024 * 1024
        ),
        name="gated_input",
    )(seg_adapter, holder_slot, seg_length, tokens, gate_weight, up_weight, adapter_in, adapter_out)


def plain(
    tokens, gate_weight, up_weight, adapter_in, adapter_out, seg_adapter, holder_slot, seg_length
):
    holders = lax.axis_size("wide")
    my_index = lax.axis_index("wide")
    held_count = adapter_in.shape[0]
    rank_size = adapter_in.shape[1]
    model_dim = tokens.shape[1]
    row_count = tokens.shape[0] * holders
    seg_count = seg_adapter.shape[0]
    seg_size = row_count // seg_count
    columns = gate_weight.shape[1]
    pool_size = holder_slot.shape[0]
    matches = seg_adapter[:, None] == jnp.arange(pool_size, dtype=jnp.int32)[None, :]
    seg_slot = jnp.sum(jnp.where(matches, holder_slot[None, :], 0), axis=1)
    seg_owner = seg_slot // held_count
    local_slot = seg_slot % held_count
    gathered = lax.all_gather(tokens, "wide", axis=0, tiled=True)
    gate_block = jnp.dot(gathered, gate_weight, preferred_element_type=jnp.float32)
    up_weight_block = jnp.dot(gathered, up_weight, preferred_element_type=jnp.float32)

    def per_segment(operand):
        seg_rows, owner_now, slot_now = operand

        def compute():
            return lax.dot_general(
                seg_rows,
                adapter_in[slot_now],
                (((1,), (1,)), ((), ())),
                preferred_element_type=jnp.float32,
            )

        def nothing():
            return jnp.zeros((seg_size, rank_size), jnp.float32)

        return lax.cond(owner_now == my_index, compute, nothing)

    seg_blocks = gathered.reshape(seg_count, seg_size, model_dim)
    partial_in = lax.map(per_segment, (seg_blocks, seg_owner, local_slot)).reshape(
        row_count, rank_size
    )
    reduced_rank_state = lax.psum(partial_in, "wide").astype(jnp.bfloat16)
    selected_output = adapter_out[seg_slot]
    adapter_term = jnp.einsum(
        "iyg,ign->iyn",
        reduced_rank_state.reshape(seg_count, seg_size, rank_size),
        selected_output,
        preferred_element_type=jnp.float32,
    ).reshape(row_count, columns)
    up_output_total = up_weight_block + adapter_scale * adapter_term
    positions = jnp.arange(seg_size, dtype=jnp.int32)
    live_rows = (positions[None, :] < seg_length[:, None]).reshape(row_count)
    hidden = jnp.where(
        live_rows[:, None], jax.nn.silu(gate_block) * up_output_total, jnp.float32(0.0)
    )
    return hidden.astype(jnp.bfloat16)


def on_device(tokens, gate_weight, up_weight, adapter_in, *rest):
    n = lax.axis_size("wide")
    own_rows, dim = tokens.shape
    resident = 2 * (2 * dim * gate_weight.shape[1] + own_rows * n * dim)
    fits = (
        n % 4 == 0
        and gate_weight.shape[1] % 128 == 0
        and own_rows % 8 == 0
        and own_rows <= 32
        and adapter_in.shape[0] == 1
        and dim % (4 * WINDOWS * PARTS * 128) == 0
        and resident < 40 * 1024 * 1024
    )
    return (fused if fits else plain)(tokens, gate_weight, up_weight, adapter_in, *rest)


def solution(mesh):
    in_specs = (
        P(("groups", "wide"), None),
        P(None, "wide"),
        P(None, "wide"),
        P(("groups", "wide"), None, None),
        P("groups", None, "wide"),
        P("groups"),
        P("groups"),
        P("groups"),
    )
    out_specs = P("groups", "wide")
    return jax.shard_map(
        on_device, mesh=mesh, in_specs=in_specs, out_specs=out_specs, check_vma=False
    )
```

```python
import functools

import jax
import jax.numpy as jnp
from jax import lax
from jax.experimental import pallas as pl
from jax.experimental.pallas import tpu as pltpu
from jax.sharding import PartitionSpec as P

adapter_scale = 0.5
MESH = pl.DeviceIdType.MESH
WINDOWS = 1
PARTS = 4


def kernel(
    n, seg_count,
    seg_adapter, holder_slot, seg_length, tokens, gate_weight, up_weight, adapter_in, adapter_out,
    hidden,
    gathered, weights, inmap, outmap, acc, low_acc, swap_out, swap_in, low_parts, low_sum,
    weight_sem, map_sem, swap_sem, ring_send, ring_recv, pair_send, pair_recv,
    low_send, low_recv, all_send, all_recv,
):
    me = lax.axis_index("wide")
    chips = n // 2
    depth = chips // 2
    steps = chips - 1
    chip, core = me // 2, me % 2
    zi, yi = chip // 2, chip % 2
    pos = zi + yi * (2 * depth - 1 - 2 * zi)
    pair = chip * 2 + 1 - core
    rows, columns = hidden.shape
    chip_rows = rows // chips
    own_rows = rows // n
    half_dim = tokens.shape[1] // 2
    width = gathered.shape[-1]
    part = width // PARTS
    seg_size = rows // seg_count
    rank = adapter_in.shape[1]
    lanes = inmap.shape[0]

    def chip_at(q):
        side = q // depth
        return (q + side * (2 * depth - 1 - 2 * q)) * 2 + side

    def block_of(half, way, win):
        return (half * 2 + way) * WINDOWS + win

    def weight_copy(mat, half, way, win):
        block = block_of(half, way, win)
        source = (gate_weight, up_weight)[mat]
        return pltpu.make_async_copy(
            source.at[pl.ds(pl.multiple_of(block * width, width), width), :],
            weights.at[mat, block],
            weight_sem.at[mat, block],
        )

    inmap_copy = pltpu.make_async_copy(
        adapter_in.at[0], inmap.at[pl.ds(0, rank), :], map_sem.at[0]
    )
    outmap_copy = pltpu.make_async_copy(adapter_out, outmap, map_sem.at[1])

    barrier = pltpu.get_barrier_semaphore()
    after = chip_at((pos + 1) % chips) * 2 + core
    before = chip_at((pos + chips - 1) % chips) * 2 + core
    for neighbour in (pair, after, before):
        pl.semaphore_signal(barrier, inc=1, device_id={"wide": neighbour}, device_id_type=MESH)
    other = tokens[:, pl.ds(pl.multiple_of((1 - core) * half_dim, half_dim), half_dim)]
    pad = jnp.zeros((swap_out.shape[0] - own_rows, half_dim), jnp.float32)
    swap_out[...] = jnp.concatenate([other.astype(jnp.float32), pad], axis=0).astype(jnp.bfloat16)
    pl.semaphore_wait(barrier, 3)

    swap = pltpu.make_async_remote_copy(
        src_ref=swap_out, dst_ref=swap_in, send_sem=swap_sem.at[0], recv_sem=swap_sem.at[1],
        device_id={"wide": pair}, device_id_type=MESH,
    )
    swap.start()
    inmap_copy.start()
    for win in range(WINDOWS):
        for half in range(2):
            for way in range(2):
                for mat in range(2):
                    weight_copy(mat, half, way, win).start()
    outmap_copy.start()
    swap.wait()

    def rows_of(origin):
        return pl.ds(pl.multiple_of(chip_at(origin) * chip_rows, 16), chip_rows)

    def ring_copy(way, win, cut, step, origin):
        sign = 1 - 2 * way
        target = chip_at((pos + sign + chips) % chips) * 2 + core
        place = gathered.at[core, way, win, rows_of(origin), pl.ds(cut * part, part)]
        return pltpu.make_async_remote_copy(
            src_ref=place, dst_ref=place,
            send_sem=ring_send.at[way, win, cut, step], recv_sem=ring_recv.at[way, win, cut, step],
            device_id={"wide": target}, device_id_type=MESH,
        )

    def pair_copy(half, way, win, step, origin):
        place = gathered.at[half, way, win, rows_of(origin), :]
        return pltpu.make_async_remote_copy(
            src_ref=place, dst_ref=place,
            send_sem=pair_send.at[way, win, step], recv_sem=pair_recv.at[way, win, step],
            device_id={"wide": pair}, device_id_type=MESH,
        )

    def origin_at(way, step):
        sign = 1 - 2 * way
        return (pos - sign * step + 2 * chips) % chips

    def send_own(win):
        for cut in range(PARTS):
            for way in range(2):
                ring_copy(way, win, cut, 0, pos).start()
        for way in range(2):
            pair_copy(core, way, win, 0, pos).start()

    for win in range(WINDOWS):
        for way in range(2):
            at = (way * WINDOWS + win) * width
            mine = tokens[:, pl.ds(pl.multiple_of(core * half_dim + at, width), width)]
            mine = mine.astype(jnp.float32)
            theirs = swap_in[:, at:at + width].astype(jnp.float32)[:own_rows]
            first = jnp.where(core == 0, mine, theirs)
            second = jnp.where(core == 0, theirs, mine)
            gathered[core, way, win, rows_of(pos), :] = jnp.concatenate(
                [first, second], axis=0
            ).astype(jnp.bfloat16)
        if win == 0:
            send_own(0)

    acc[...] = jnp.zeros_like(acc)
    low_acc[...] = jnp.zeros_like(low_acc)
    if lanes > rank:
        inmap[rank:, :] = jnp.zeros((lanes - rank, inmap.shape[1]), inmap.dtype)
    inmap_copy.wait()

    def wait_pair(way, win):
        def one(step, carry):
            pair_copy(1 - core, way, win, step, origin_at(way, step)).wait_recv()
            return carry
        lax.fori_loop(0, chips, one, 0)

    def low_piece(win, half, way):
        at = pl.multiple_of(block_of(half, way, win) * width, width)
        low_acc[...] += lax.dot_general(
            gathered[half, way, win], inmap[:, pl.ds(at, width)],
            (((1,), (1,)), ((), ())), preferred_element_type=jnp.float32,
        )

    def main_piece(win, index, with_low):
        mat, way, half = index % 2, (index // 2) % 2, (core + index // 4) % 2
        block = block_of(half, way, win)
        if with_low:
            @pl.when((mat == 0) & (index >= 4))
            def _():
                wait_pair(way, win)

            @pl.when(mat == 0)
            def _():
                low_piece(win, half, way)
        pltpu.make_async_copy(
            gate_weight.at[pl.ds(0, width), :], weights.at[mat, block], weight_sem.at[mat, block]
        ).wait()
        acc[mat] += jnp.dot(
            gathered[half, way, win], weights[mat, block], preferred_element_type=jnp.float32
        )

    def round_of(t, carry):
        win, step = t // steps, t % steps
        for cut in range(PARTS):
            for way in range(2):
                origin = origin_at(way, step + 1)
                ring_copy(way, win, cut, step, origin).wait_recv()

                @pl.when(step < steps - 1)
                def _():
                    ring_copy(way, win, cut, step + 1, origin).start()
        for way in range(2):
            pair_copy(core, way, win, step + 1, origin_at(way, step + 1)).start()

        @pl.when((step == steps - 2) & (win < WINDOWS - 1))
        def _():
            send_own(win + 1)

        @pl.when(win > 0)
        def _():
            first = (step * 8) // steps
            count = ((step + 1) * 8) // steps - first

            def piece(i, c):
                main_piece(win - 1, first + i, True)
                return c
            lax.fori_loop(0, count, piece, 0)
        return carry

    lax.fori_loop(0, WINDOWS * steps, round_of, 0)

    last = WINDOWS - 1
    for way in range(2):
        low_piece(last, core, way)
    for way in range(2):
        wait_pair(way, last)
        low_piece(last, 1 - core, way)

    slots = [holder_slot[seg_adapter[s]] for s in range(seg_count)]
    kept = jnp.concatenate(
        [
            jnp.where(slots[s] == me, low_acc[s * seg_size:(s + 1) * seg_size, :], 0.0)
            for s in range(seg_count)
        ],
        axis=0,
    )
    low_acc[...] = kept

    def own_slice(device):
        return pl.ds(pl.multiple_of(device * own_rows, 8), own_rows)

    def low_copy(i):
        target = lax.rem(me + i, n)
        return pltpu.make_async_remote_copy(
            src_ref=low_acc.at[own_slice(target), :], dst_ref=low_parts.at[i],
            send_sem=low_send.at[i], recv_sem=low_recv.at[i],
            device_id={"wide": target}, device_id_type=MESH,
        )

    def all_copy(i):
        target = lax.rem(me + i, n)
        place = low_sum.at[own_slice(me), :]
        return pltpu.make_async_remote_copy(
            src_ref=place, dst_ref=place, send_sem=all_send.at[i], recv_sem=all_recv.at[i],
            device_id={"wide": target}, device_id_type=MESH,
        )

    def all_arrived(i):
        place = low_sum.at[own_slice(lax.rem(me + n - i, n)), :]
        return pltpu.make_async_remote_copy(
            src_ref=place, dst_ref=place, send_sem=all_send.at[i], recv_sem=all_recv.at[i],
            device_id={"wide": lax.rem(me + i, n)}, device_id_type=MESH,
        )

    for i in range(1, n):
        low_copy(i).start()

    def early(i, c):
        main_piece(last, i, False)
        return c

    lax.fori_loop(0, 4, early, 0)
    for i in range(1, n):
        low_copy(i).wait_recv()
    total = low_acc[own_slice(me), :]
    for i in range(1, n):
        total = total + low_parts[i]
    low_sum[own_slice(me), :] = total
    for i in range(1, n):
        all_copy(i).start()
    lax.fori_loop(4, 8, early, 0)
    acc[0] = acc[0] / (1.0 + jnp.exp(-acc[0]))
    outmap_copy.wait()
    for i in range(1, n):
        all_arrived(i).wait_recv()
    for s in range(seg_count):
        at = s * seg_size
        low = low_sum[at:at + seg_size, :rank].astype(jnp.bfloat16)
        term = jnp.dot(low, outmap[slots[s]], preferred_element_type=jnp.float32)
        value = acc[0, at:at + seg_size, :] * (
            acc[1, at:at + seg_size, :] + adapter_scale * term
        )
        position = lax.broadcasted_iota(jnp.int32, value.shape, 0)
        hidden[at:at + seg_size, :] = jnp.where(
            position < seg_length[s], value, 0.0
        ).astype(hidden.dtype)

    for i in range(1, n):
        low_copy(i).wait_send()
        all_copy(i).wait_send()

    def drain(t, carry):
        win, step = t // steps, t % steps
        for way in range(2):
            for cut in range(PARTS):
                ring_copy(way, win, cut, step, pos).wait_send()
            pair_copy(core, way, win, step, pos).wait_send()

            @pl.when(step == 0)
            def _():
                pair_copy(core, way, win, steps, pos).wait_send()
        return carry

    lax.fori_loop(0, WINDOWS * steps, drain, 0)


def fused(
    tokens, gate_weight, up_weight, adapter_in, adapter_out, seg_adapter, holder_slot, seg_length
):
    n = lax.axis_size("wide")
    rows = tokens.shape[0] * n
    dim = tokens.shape[1]
    columns = gate_weight.shape[1]
    lanes = -(-adapter_in.shape[1] // 128) * 128
    chips = n // 2
    width = dim // 4 // WINDOWS
    dma = pltpu.SemaphoreType.DMA
    smem = pl.BlockSpec(memory_space=pltpu.SMEM)
    hbm = pl.BlockSpec(memory_space=pl.ANY)
    vmem = pl.BlockSpec(memory_space=pltpu.VMEM)
    return pl.pallas_call(
        functools.partial(kernel, n, seg_adapter.shape[0]),
        out_shape=jax.ShapeDtypeStruct((rows, columns), jnp.bfloat16),
        in_specs=[smem, smem, smem, vmem, hbm, hbm, hbm, hbm],
        out_specs=vmem,
        scratch_shapes=[
            pltpu.VMEM((2, 2, WINDOWS, rows, width), jnp.bfloat16),
            pltpu.VMEM((2, 4 * WINDOWS, width, columns), jnp.bfloat16),
            pltpu.VMEM((lanes, dim), jnp.bfloat16),
            pltpu.VMEM(adapter_out.shape, jnp.bfloat16),
            pltpu.VMEM((2, rows, columns), jnp.float32),
            pltpu.VMEM((rows, lanes), jnp.float32),
            pltpu.VMEM((32, dim // 2), jnp.bfloat16),
            pltpu.VMEM((32, dim // 2), jnp.bfloat16),
            pltpu.VMEM((n, rows // n, lanes), jnp.float32),
            pltpu.VMEM((rows, lanes), jnp.float32),
            dma((2, 4 * WINDOWS)),
            dma((2,)),
            dma((2,)),
            dma((2, WINDOWS, PARTS, chips - 1)),
            dma((2, WINDOWS, PARTS, chips - 1)),
            dma((2, WINDOWS, chips)),
            dma((2, WINDOWS, chips)),
            dma((n,)),
            dma((n,)),
            dma((n,)),
            dma((n,)),
        ],
        compiler_params=pltpu.CompilerParams(
            collective_id=0, has_side_effects=True, vmem_limit_bytes=60 * 1024 * 1024
        ),
        name="gated_input",
    )(seg_adapter, holder_slot, seg_length, tokens, gate_weight, up_weight, adapter_in, adapter_out)


def plain(
    tokens, gate_weight, up_weight, adapter_in, adapter_out, seg_adapter, holder_slot, seg_length
):
    holders = lax.axis_size("wide")
    my_index = lax.axis_index("wide")
    held_count = adapter_in.shape[0]
    rank_size = adapter_in.shape[1]
    model_dim = tokens.shape[1]
    row_count = tokens.shape[0] * holders
    seg_count = seg_adapter.shape[0]
    seg_size = row_count // seg_count
    columns = gate_weight.shape[1]
    pool_size = holder_slot.shape[0]
    matches = seg_adapter[:, None] == jnp.arange(pool_size, dtype=jnp.int32)[None, :]
    seg_slot = jnp.sum(jnp.where(matches, holder_slot[None, :], 0), axis=1)
    seg_owner = seg_slot // held_count
    local_slot = seg_slot % held_count
    gathered = lax.all_gather(tokens, "wide", axis=0, tiled=True)
    gate_block = jnp.dot(gathered, gate_weight, preferred_element_type=jnp.float32)
    up_weight_block = jnp.dot(gathered, up_weight, preferred_element_type=jnp.float32)

    def per_segment(operand):
        seg_rows, owner_now, slot_now = operand

        def compute():
            return lax.dot_general(
                seg_rows,
                adapter_in[slot_now],
                (((1,), (1,)), ((), ())),
                preferred_element_type=jnp.float32,
            )

        def nothing():
            return jnp.zeros((seg_size, rank_size), jnp.float32)

        return lax.cond(owner_now == my_index, compute, nothing)

    seg_blocks = gathered.reshape(seg_count, seg_size, model_dim)
    partial_in = lax.map(per_segment, (seg_blocks, seg_owner, local_slot)).reshape(
        row_count, rank_size
    )
    reduced_rank_state = lax.psum(partial_in, "wide").astype(jnp.bfloat16)
    selected_output = adapter_out[seg_slot]
    adapter_term = jnp.einsum(
        "iyg,ign->iyn",
        reduced_rank_state.reshape(seg_count, seg_size, rank_size),
        selected_output,
        preferred_element_type=jnp.float32,
    ).reshape(row_count, columns)
    up_output_total = up_weight_block + adapter_scale * adapter_term
    positions = jnp.arange(seg_size, dtype=jnp.int32)
    live_rows = (positions[None, :] < seg_length[:, None]).reshape(row_count)
    hidden = jnp.where(
        live_rows[:, None], jax.nn.silu(gate_block) * up_output_total, jnp.float32(0.0)
    )
    return hidden.astype(jnp.bfloat16)


def on_device(tokens, gate_weight, up_weight, adapter_in, *rest):
    n = lax.axis_size("wide")
    own_rows, dim = tokens.shape
    resident = 2 * (2 * dim * gate_weight.shape[1] + own_rows * n * dim)
    fits = (
        n % 4 == 0
        and gate_weight.shape[1] % 128 == 0
        and own_rows % 8 == 0
        and own_rows <= 32
        and adapter_in.shape[0] == 1
        and dim % (4 * WINDOWS * PARTS * 128) == 0
        and resident < 40 * 1024 * 1024
    )
    return (fused if fits else plain)(tokens, gate_weight, up_weight, adapter_in, *rest)


def solution(mesh):
    in_specs = (
        P(("groups", "wide"), None),
        P(None, "wide"),
        P(None, "wide"),
        P(("groups", "wide"), None, None),
        P("groups", None, "wide"),
        P("groups"),
        P("groups"),
        P("groups"),
    )
    out_specs = P("groups", "wide")
    return jax.shard_map(
        on_device, mesh=mesh, in_specs=in_specs, out_specs=out_specs, check_vma=False
    )
```

```python
import functools

import jax
import jax.numpy as jnp
from jax import lax
from jax.experimental import pallas as pl
from jax.experimental.pallas import tpu as pltpu
from jax.sharding import PartitionSpec as P

adapter_scale = 0.5
MESH = pl.DeviceIdType.MESH
WINDOWS = 1
PARTS = 4


def kernel(
    n, seg_count,
    seg_adapter, holder_slot, seg_length, tokens, gate_weight, up_weight, adapter_in, adapter_out,
    hidden,
    gathered, weights, inmap, outmap, acc, low_acc, swap_out, swap_in, low_parts, low_sum,
    weight_sem, map_sem, swap_sem, ring_send, ring_recv, pair_send, pair_recv,
    low_send, low_recv, all_send, all_recv,
):
    me = lax.axis_index("wide")
    chips = n // 2
    depth = chips // 2
    steps = chips - 1
    chip, core = me // 2, me % 2
    zi, yi = chip // 2, chip % 2
    pos = zi + yi * (2 * depth - 1 - 2 * zi)
    pair = chip * 2 + 1 - core
    rows, columns = hidden.shape
    chip_rows = rows // chips
    own_rows = rows // n
    half_dim = tokens.shape[1] // 2
    width = gathered.shape[-1]
    part = width // PARTS
    seg_size = rows // seg_count
    rank = adapter_in.shape[1]
    lanes = inmap.shape[0]

    def chip_at(q):
        side = q // depth
        return (q + side * (2 * depth - 1 - 2 * q)) * 2 + side

    def block_of(half, way, win):
        return (half * 2 + way) * WINDOWS + win

    def weight_copy(mat, half, way, win):
        block = block_of(half, way, win)
        source = (gate_weight, up_weight)[mat]
        return pltpu.make_async_copy(
            source.at[pl.ds(pl.multiple_of(block * width, width), width), :],
            weights.at[mat, block],
            weight_sem.at[mat, block],
        )

    inmap_copy = pltpu.make_async_copy(
        adapter_in.at[0], inmap.at[pl.ds(0, rank), :], map_sem.at[0]
    )
    outmap_copy = pltpu.make_async_copy(adapter_out, outmap, map_sem.at[1])

    barrier = pltpu.get_barrier_semaphore()
    after = chip_at((pos + 1) % chips) * 2 + core
    before = chip_at((pos + chips - 1) % chips) * 2 + core
    for neighbour in (pair, after, before):
        pl.semaphore_signal(barrier, inc=1, device_id={"wide": neighbour}, device_id_type=MESH)
    other = tokens[:, pl.ds(pl.multiple_of((1 - core) * half_dim, half_dim), half_dim)]
    pad = jnp.zeros((swap_out.shape[0] - own_rows, half_dim), jnp.float32)
    swap_out[...] = jnp.concatenate([other.astype(jnp.float32), pad], axis=0).astype(jnp.bfloat16)
    pl.semaphore_wait(barrier, 3)

    swap = pltpu.make_async_remote_copy(
        src_ref=swap_out, dst_ref=swap_in, send_sem=swap_sem.at[0], recv_sem=swap_sem.at[1],
        device_id={"wide": pair}, device_id_type=MESH,
    )
    swap.start()
    inmap_copy.start()
    for win in range(WINDOWS):
        for half in range(2):
            for way in range(2):
                for mat in range(2):
                    weight_copy(mat, half, way, win).start()
    outmap_copy.start()
    swap.wait()

    def rows_of(origin):
        return pl.ds(pl.multiple_of(chip_at(origin) * chip_rows, 16), chip_rows)

    def slot_rows(slot):
        return pl.ds(pl.multiple_of(slot * chip_rows, 16), chip_rows)

    def ring_copy(way, win, cut, step):
        columns_of = pl.ds(cut * part, part)
        return pltpu.make_async_remote_copy(
            src_ref=gathered.at[core, way, win, slot_rows(step), columns_of],
            dst_ref=gathered.at[core, way, win, slot_rows(step + 1), columns_of],
            send_sem=ring_send.at[way, win, cut, step], recv_sem=ring_recv.at[way, win, cut, step],
            device_id={"wide": (after, before)[way]}, device_id_type=MESH,
        )

    def pair_copy(half, way, win, step):
        place = gathered.at[half, way, win, slot_rows(step), :]
        return pltpu.make_async_remote_copy(
            src_ref=place, dst_ref=place,
            send_sem=pair_send.at[way, win, step], recv_sem=pair_recv.at[way, win, step],
            device_id={"wide": pair}, device_id_type=MESH,
        )

    def origin_at(way, step):
        sign = 1 - 2 * way
        return (pos - sign * step + 2 * chips) % chips

    def send_own(win):
        for cut in range(PARTS):
            for way in range(2):
                ring_copy(way, win, cut, 0).start()
        for way in range(2):
            pair_copy(core, way, win, 0).start()

    for win in range(WINDOWS):
        for way in range(2):
            at = (way * WINDOWS + win) * width
            mine = tokens[:, pl.ds(pl.multiple_of(core * half_dim + at, width), width)]
            mine = mine.astype(jnp.float32)
            theirs = swap_in[:, at:at + width].astype(jnp.float32)[:own_rows]
            first = jnp.where(core == 0, mine, theirs)
            second = jnp.where(core == 0, theirs, mine)
            gathered[core, way, win, :chip_rows, :] = jnp.concatenate(
                [first, second], axis=0
            ).astype(jnp.bfloat16)
        if win == 0:
            send_own(0)

    acc[...] = jnp.zeros_like(acc)
    low_acc[...] = jnp.zeros_like(low_acc)
    if lanes > rank:
        inmap[rank:, :] = jnp.zeros((lanes - rank, inmap.shape[1]), inmap.dtype)
    inmap_copy.wait()

    group = chips // 2

    def group_slots(which):
        return pl.ds(pl.multiple_of(which * group * chip_rows, 16), group * chip_rows)

    def wait_pair(which, way):
        for k in range(group):
            pair_copy(1 - core, way, 0, which * group + k).wait_recv()

    def add_rows(target, which, way, value):
        for k in range(group):
            target[rows_of(origin_at(way, which * group + k)), :] += (
                value[k * chip_rows:(k + 1) * chip_rows]
            )

    def low_piece(which, half, way):
        at = pl.multiple_of(block_of(half, way, 0) * width, width)
        value = lax.dot_general(
            gathered[half, way, 0, group_slots(which), :], inmap[:, pl.ds(at, width)],
            (((1,), (1,)), ((), ())), preferred_element_type=jnp.float32,
        )
        add_rows(low_acc, which, way, value)

    def main_piece(which, index, first):
        mat, way, half = index % 2, (index // 2) % 2, (core + index // 4) % 2
        block = block_of(half, way, 0)
        if first:
            @pl.when((mat == 0) & (index >= 4))
            def _():
                wait_pair(which, way)

            @pl.when(mat == 0)
            def _():
                low_piece(which, half, way)
            pltpu.make_async_copy(
                gate_weight.at[pl.ds(0, width), :], weights.at[mat, block],
                weight_sem.at[mat, block],
            ).wait()
        value = jnp.dot(
            gathered[half, way, 0, group_slots(which), :], weights[mat, block],
            preferred_element_type=jnp.float32,
        )
        add_rows(acc.at[mat], which, way, value)

    per_round = -(-8 // (steps - group + 1))

    def round_of(step, carry):
        for turn in range(2):
            for cut in range(turn * PARTS // 2, (turn + 1) * PARTS // 2):
                for way in range(2):
                    ring_copy(way, 0, cut, step).wait_recv()

                    @pl.when(step < steps - 1)
                    def _():
                        ring_copy(way, 0, cut, step + 1).start()
            if turn == 1:
                for way in range(2):
                    pair_copy(core, way, 0, step + 1).start()

            @pl.when(step >= group - 1)
            def _():
                begin = (step - group + 1) * per_round + turn * (per_round // 2)
                count = per_round - per_round // 2 if turn else per_round // 2

                def piece(i, c):
                    @pl.when(begin + i < 8)
                    def _():
                        main_piece(0, begin + i, True)
                    return c
                @pl.when((step < steps - 1) | (turn == 0))
                def _():
                    lax.fori_loop(0, count, piece, 0)
        return carry

    lax.fori_loop(0, steps, round_of, 0)

    for way in range(2):
        low_piece(1, core, way)
    for way in range(2):
        wait_pair(1, way)
        low_piece(1, 1 - core, way)

    slots = [holder_slot[seg_adapter[s]] for s in range(seg_count)]
    kept = jnp.concatenate(
        [
            jnp.where(slots[s] == me, low_acc[s * seg_size:(s + 1) * seg_size, :], 0.0)
            for s in range(seg_count)
        ],
        axis=0,
    )
    low_acc[...] = kept

    def own_slice(device):
        return pl.ds(pl.multiple_of(device * own_rows, 8), own_rows)

    def low_copy(i):
        target = lax.rem(me + i, n)
        return pltpu.make_async_remote_copy(
            src_ref=low_acc.at[own_slice(target), :], dst_ref=low_parts.at[i],
            send_sem=low_send.at[i], recv_sem=low_recv.at[i],
            device_id={"wide": target}, device_id_type=MESH,
        )

    def all_copy(i):
        target = lax.rem(me + i, n)
        place = low_sum.at[own_slice(me), :]
        return pltpu.make_async_remote_copy(
            src_ref=place, dst_ref=place, send_sem=all_send.at[i], recv_sem=all_recv.at[i],
            device_id={"wide": target}, device_id_type=MESH,
        )

    def all_arrived(i):
        place = low_sum.at[own_slice(lax.rem(me + n - i, n)), :]
        return pltpu.make_async_remote_copy(
            src_ref=place, dst_ref=place, send_sem=all_send.at[i], recv_sem=all_recv.at[i],
            device_id={"wide": lax.rem(me + i, n)}, device_id_type=MESH,
        )

    for i in range(1, n):
        low_copy(i).start()
    main_piece(0, 7, True)

    def early(i, c):
        main_piece(1, i, False)
        return c

    lax.fori_loop(0, 4, early, 0)
    for i in range(1, n):
        low_copy(i).wait_recv()
    total = low_acc[own_slice(me), :]
    for i in range(1, n):
        total = total + low_parts[i]
    low_sum[own_slice(me), :] = total
    for i in range(1, n):
        all_copy(i).start()
    lax.fori_loop(4, 8, early, 0)
    acc[0] = acc[0] / (1.0 + jnp.exp(-acc[0]))
    outmap_copy.wait()
    for i in range(1, n):
        all_arrived(i).wait_recv()
    for s in range(seg_count):
        at = s * seg_size
        low = low_sum[at:at + seg_size, :rank].astype(jnp.bfloat16)
        term = jnp.dot(low, outmap[slots[s]], preferred_element_type=jnp.float32)
        value = acc[0, at:at + seg_size, :] * (
            acc[1, at:at + seg_size, :] + adapter_scale * term
        )
        position = lax.broadcasted_iota(jnp.int32, value.shape, 0)
        hidden[at:at + seg_size, :] = jnp.where(
            position < seg_length[s], value, 0.0
        ).astype(hidden.dtype)

    for i in range(1, n):
        low_copy(i).wait_send()
        all_copy(i).wait_send()

    def drain(t, carry):
        win, step = t // steps, t % steps
        for way in range(2):
            for cut in range(PARTS):
                ring_copy(way, win, cut, step).wait_send()
            pair_copy(core, way, win, step).wait_send()

            @pl.when(step == 0)
            def _():
                pair_copy(core, way, win, steps).wait_send()
        return carry

    lax.fori_loop(0, WINDOWS * steps, drain, 0)


def fused(
    tokens, gate_weight, up_weight, adapter_in, adapter_out, seg_adapter, holder_slot, seg_length
):
    n = lax.axis_size("wide")
    rows = tokens.shape[0] * n
    dim = tokens.shape[1]
    columns = gate_weight.shape[1]
    lanes = -(-adapter_in.shape[1] // 128) * 128
    chips = n // 2
    width = dim // 4 // WINDOWS
    dma = pltpu.SemaphoreType.DMA
    smem = pl.BlockSpec(memory_space=pltpu.SMEM)
    hbm = pl.BlockSpec(memory_space=pl.ANY)
    vmem = pl.BlockSpec(memory_space=pltpu.VMEM)
    return pl.pallas_call(
        functools.partial(kernel, n, seg_adapter.shape[0]),
        out_shape=jax.ShapeDtypeStruct((rows, columns), jnp.bfloat16),
        in_specs=[smem, smem, smem, vmem, hbm, hbm, hbm, hbm],
        out_specs=vmem,
        scratch_shapes=[
            pltpu.VMEM((2, 2, WINDOWS, rows, width), jnp.bfloat16),
            pltpu.VMEM((2, 4 * WINDOWS, width, columns), jnp.bfloat16),
            pltpu.VMEM((lanes, dim), jnp.bfloat16),
            pltpu.VMEM(adapter_out.shape, jnp.bfloat16),
            pltpu.VMEM((2, rows, columns), jnp.float32),
            pltpu.VMEM((rows, lanes), jnp.float32),
            pltpu.VMEM((32, dim // 2), jnp.bfloat16),
            pltpu.VMEM((32, dim // 2), jnp.bfloat16),
            pltpu.VMEM((n, rows // n, lanes), jnp.float32),
            pltpu.VMEM((rows, lanes), jnp.float32),
            dma((2, 4 * WINDOWS)),
            dma((2,)),
            dma((2,)),
            dma((2, WINDOWS, PARTS, chips - 1)),
            dma((2, WINDOWS, PARTS, chips - 1)),
            dma((2, WINDOWS, chips)),
            dma((2, WINDOWS, chips)),
            dma((n,)),
            dma((n,)),
            dma((n,)),
            dma((n,)),
        ],
        compiler_params=pltpu.CompilerParams(
            collective_id=0, has_side_effects=True, vmem_limit_bytes=60 * 1024 * 1024
        ),
        name="gated_input",
    )(seg_adapter, holder_slot, seg_length, tokens, gate_weight, up_weight, adapter_in, adapter_out)


def plain(
    tokens, gate_weight, up_weight, adapter_in, adapter_out, seg_adapter, holder_slot, seg_length
):
    holders = lax.axis_size("wide")
    my_index = lax.axis_index("wide")
    held_count = adapter_in.shape[0]
    rank_size = adapter_in.shape[1]
    model_dim = tokens.shape[1]
    row_count = tokens.shape[0] * holders
    seg_count = seg_adapter.shape[0]
    seg_size = row_count // seg_count
    columns = gate_weight.shape[1]
    pool_size = holder_slot.shape[0]
    matches = seg_adapter[:, None] == jnp.arange(pool_size, dtype=jnp.int32)[None, :]
    seg_slot = jnp.sum(jnp.where(matches, holder_slot[None, :], 0), axis=1)
    seg_owner = seg_slot // held_count
    local_slot = seg_slot % held_count
    gathered = lax.all_gather(tokens, "wide", axis=0, tiled=True)
    gate_block = jnp.dot(gathered, gate_weight, preferred_element_type=jnp.float32)
    up_weight_block = jnp.dot(gathered, up_weight, preferred_element_type=jnp.float32)

    def per_segment(operand):
        seg_rows, owner_now, slot_now = operand

        def compute():
            return lax.dot_general(
                seg_rows,
                adapter_in[slot_now],
                (((1,), (1,)), ((), ())),
                preferred_element_type=jnp.float32,
            )

        def nothing():
            return jnp.zeros((seg_size, rank_size), jnp.float32)

        return lax.cond(owner_now == my_index, compute, nothing)

    seg_blocks = gathered.reshape(seg_count, seg_size, model_dim)
    partial_in = lax.map(per_segment, (seg_blocks, seg_owner, local_slot)).reshape(
        row_count, rank_size
    )
    reduced_rank_state = lax.psum(partial_in, "wide").astype(jnp.bfloat16)
    selected_output = adapter_out[seg_slot]
    adapter_term = jnp.einsum(
        "iyg,ign->iyn",
        reduced_rank_state.reshape(seg_count, seg_size, rank_size),
        selected_output,
        preferred_element_type=jnp.float32,
    ).reshape(row_count, columns)
    up_output_total = up_weight_block + adapter_scale * adapter_term
    positions = jnp.arange(seg_size, dtype=jnp.int32)
    live_rows = (positions[None, :] < seg_length[:, None]).reshape(row_count)
    hidden = jnp.where(
        live_rows[:, None], jax.nn.silu(gate_block) * up_output_total, jnp.float32(0.0)
    )
    return hidden.astype(jnp.bfloat16)


def on_device(tokens, gate_weight, up_weight, adapter_in, *rest):
    n = lax.axis_size("wide")
    own_rows, dim = tokens.shape
    resident = 2 * (2 * dim * gate_weight.shape[1] + own_rows * n * dim)
    fits = (
        n % 4 == 0
        and gate_weight.shape[1] % 128 == 0
        and own_rows % 8 == 0
        and own_rows <= 32
        and adapter_in.shape[0] == 1
        and dim % (4 * WINDOWS * PARTS * 128) == 0
        and resident < 40 * 1024 * 1024
    )
    return (fused if fits else plain)(tokens, gate_weight, up_weight, adapter_in, *rest)


def solution(mesh):
    in_specs = (
        P(("groups", "wide"), None),
        P(None, "wide"),
        P(None, "wide"),
        P(("groups", "wide"), None, None),
        P("groups", None, "wide"),
        P("groups"),
        P("groups"),
        P("groups"),
    )
    out_specs = P("groups", "wide")
    return jax.shard_map(
        on_device, mesh=mesh, in_specs=in_specs, out_specs=out_specs, check_vma=False
    )
```

```python
import functools

import jax
import jax.numpy as jnp
from jax import lax
from jax.experimental import pallas as pl
from jax.experimental.pallas import tpu as pltpu
from jax.sharding import PartitionSpec as P

adapter_scale = 0.5
MESH = pl.DeviceIdType.MESH
WINDOWS = 1
PARTS = 4


def kernel(
    n, seg_count,
    seg_adapter, holder_slot, seg_length, tokens, gate_weight, up_weight, adapter_in, adapter_out,
    hidden,
    gathered, weights, inmap, outmap, acc, low_acc, swap_out, swap_in, low_parts, low_sum,
    weight_sem, map_sem, swap_sem, ring_send, ring_recv, pair_send, pair_recv,
    low_send, low_recv, all_send, all_recv,
):
    me = lax.axis_index("wide")
    chips = n // 2
    depth = chips // 2
    steps = chips - 1
    chip, core = me // 2, me % 2
    zi, yi = chip // 2, chip % 2
    pos = zi + yi * (2 * depth - 1 - 2 * zi)
    pair = chip * 2 + 1 - core
    rows, columns = hidden.shape
    chip_rows = rows // chips
    own_rows = rows // n
    half_dim = tokens.shape[1] // 2
    width = gathered.shape[-1]
    part = width // PARTS
    seg_size = rows // seg_count
    rank = adapter_in.shape[1]
    lanes = inmap.shape[0]

    def chip_at(q):
        side = q // depth
        return (q + side * (2 * depth - 1 - 2 * q)) * 2 + side

    def block_of(half, way, win):
        return (half * 2 + way) * WINDOWS + win

    def weight_copy(mat, half, way, win):
        block = block_of(half, way, win)
        source = (gate_weight, up_weight)[mat]
        return pltpu.make_async_copy(
            source.at[pl.ds(pl.multiple_of(block * width, width), width), :],
            weights.at[mat, block],
            weight_sem.at[mat, block],
        )

    inmap_copy = pltpu.make_async_copy(
        adapter_in.at[0], inmap.at[pl.ds(0, rank), :], map_sem.at[0]
    )
    outmap_copy = pltpu.make_async_copy(adapter_out, outmap, map_sem.at[1])

    barrier = pltpu.get_barrier_semaphore()
    after = chip_at((pos + 1) % chips) * 2 + core
    before = chip_at((pos + chips - 1) % chips) * 2 + core
    for neighbour in (pair, after, before):
        pl.semaphore_signal(barrier, inc=1, device_id={"wide": neighbour}, device_id_type=MESH)
    other = tokens[:, pl.ds(pl.multiple_of((1 - core) * half_dim, half_dim), half_dim)]
    pad = jnp.zeros((swap_out.shape[0] - own_rows, half_dim), jnp.float32)
    swap_out[...] = jnp.concatenate([other.astype(jnp.float32), pad], axis=0).astype(jnp.bfloat16)
    pl.semaphore_wait(barrier, 3)

    swap = pltpu.make_async_remote_copy(
        src_ref=swap_out, dst_ref=swap_in, send_sem=swap_sem.at[0], recv_sem=swap_sem.at[1],
        device_id={"wide": pair}, device_id_type=MESH,
    )
    swap.start()
    inmap_copy.start()
    for win in range(WINDOWS):
        for half in range(2):
            for way in range(2):
                for mat in range(2):
                    weight_copy(mat, half, way, win).start()
    outmap_copy.start()
    swap.wait()

    def rows_of(origin):
        return pl.ds(pl.multiple_of(chip_at(origin) * chip_rows, 16), chip_rows)

    def slot_rows(slot):
        return pl.ds(pl.multiple_of(slot * chip_rows, 16), chip_rows)

    def ring_copy(way, win, cut, step):
        columns_of = pl.ds(cut * part, part)
        return pltpu.make_async_remote_copy(
            src_ref=gathered.at[core, way, win, slot_rows(step), columns_of],
            dst_ref=gathered.at[core, way, win, slot_rows(step + 1), columns_of],
            send_sem=ring_send.at[way, win, cut, step], recv_sem=ring_recv.at[way, win, cut, step],
            device_id={"wide": (after, before)[way]}, device_id_type=MESH,
        )

    def pair_copy(half, way, win, step):
        place = gathered.at[half, way, win, slot_rows(step), :]
        return pltpu.make_async_remote_copy(
            src_ref=place, dst_ref=place,
            send_sem=pair_send.at[way, win, step], recv_sem=pair_recv.at[way, win, step],
            device_id={"wide": pair}, device_id_type=MESH,
        )

    def origin_at(way, step):
        sign = 1 - 2 * way
        return (pos - sign * step + 2 * chips) % chips

    def send_own(way):
        for cut in range(PARTS):
            ring_copy(way, 0, cut, 0).start()
        pair_copy(core, way, 0, 0).start()

    for win in range(WINDOWS):
        for way in range(2):
            at = (way * WINDOWS + win) * width
            mine = tokens[:, pl.ds(pl.multiple_of(core * half_dim + at, width), width)]
            mine = mine.astype(jnp.float32)
            theirs = swap_in[:, at:at + width].astype(jnp.float32)[:own_rows]
            first = jnp.where(core == 0, mine, theirs)
            second = jnp.where(core == 0, theirs, mine)
            gathered[core, way, win, :chip_rows, :] = jnp.concatenate(
                [first, second], axis=0
            ).astype(jnp.bfloat16)
            send_own(way)

    acc[...] = jnp.zeros_like(acc)
    low_acc[...] = jnp.zeros_like(low_acc)
    if lanes > rank:
        inmap[rank:, :] = jnp.zeros((lanes - rank, inmap.shape[1]), inmap.dtype)
    inmap_copy.wait()

    group = chips // 2

    def group_slots(which):
        return pl.ds(pl.multiple_of(which * group * chip_rows, 16), group * chip_rows)

    def wait_pair(which, way):
        for k in range(group):
            pair_copy(1 - core, way, 0, which * group + k).wait_recv()

    def add_rows(target, which, way, value):
        for k in range(group):
            target[rows_of(origin_at(way, which * group + k)), :] += (
                value[k * chip_rows:(k + 1) * chip_rows]
            )

    def low_piece(which, half, way):
        at = pl.multiple_of(block_of(half, way, 0) * width, width)
        value = lax.dot_general(
            gathered[half, way, 0, group_slots(which), :], inmap[:, pl.ds(at, width)],
            (((1,), (1,)), ((), ())), preferred_element_type=jnp.float32,
        )
        add_rows(low_acc, which, way, value)

    def main_piece(which, index, first):
        mat, way, half = index % 2, (index // 2) % 2, (core + index // 4) % 2
        block = block_of(half, way, 0)
        if first:
            @pl.when((mat == 0) & (index >= 4))
            def _():
                wait_pair(which, way)

            @pl.when(mat == 0)
            def _():
                low_piece(which, half, way)
            pltpu.make_async_copy(
                gate_weight.at[pl.ds(0, width), :], weights.at[mat, block],
                weight_sem.at[mat, block],
            ).wait()
        value = jnp.dot(
            gathered[half, way, 0, group_slots(which), :], weights[mat, block],
            preferred_element_type=jnp.float32,
        )
        add_rows(acc.at[mat], which, way, value)

    per_round = -(-8 // (steps - group + 1))

    def round_of(step, carry):
        for turn in range(2):
            for cut in range(turn * PARTS // 2, (turn + 1) * PARTS // 2):
                for way in range(2):
                    ring_copy(way, 0, cut, step).wait_recv()

                    @pl.when(step < steps - 1)
                    def _():
                        ring_copy(way, 0, cut, step + 1).start()
            if turn == 1:
                for way in range(2):
                    pair_copy(core, way, 0, step + 1).start()

            @pl.when(step >= group - 1)
            def _():
                begin = (step - group + 1) * per_round + turn * (per_round // 2)
                count = per_round - per_round // 2 if turn else per_round // 2

                def piece(i, c):
                    @pl.when(begin + i < 8)
                    def _():
                        main_piece(0, begin + i, True)
                    return c
                @pl.when((step < steps - 1) | (turn == 0))
                def _():
                    lax.fori_loop(0, count, piece, 0)
        return carry

    lax.fori_loop(0, steps, round_of, 0)

    for way in range(2):
        low_piece(1, core, way)
    for way in range(2):
        wait_pair(1, way)
        low_piece(1, 1 - core, way)

    slots = [holder_slot[seg_adapter[s]] for s in range(seg_count)]
    kept = jnp.concatenate(
        [
            jnp.where(slots[s] == me, low_acc[s * seg_size:(s + 1) * seg_size, :], 0.0)
            for s in range(seg_count)
        ],
        axis=0,
    )
    low_acc[...] = kept

    def own_slice(device):
        return pl.ds(pl.multiple_of(device * own_rows, 8), own_rows)

    def low_copy(i):
        target = lax.rem(me + i, n)
        return pltpu.make_async_remote_copy(
            src_ref=low_acc.at[own_slice(target), :], dst_ref=low_parts.at[i],
            send_sem=low_send.at[i], recv_sem=low_recv.at[i],
            device_id={"wide": target}, device_id_type=MESH,
        )

    def all_copy(i):
        target = lax.rem(me + i, n)
        place = low_sum.at[own_slice(me), :]
        return pltpu.make_async_remote_copy(
            src_ref=place, dst_ref=place, send_sem=all_send.at[i], recv_sem=all_recv.at[i],
            device_id={"wide": target}, device_id_type=MESH,
        )

    def all_arrived(i):
        place = low_sum.at[own_slice(lax.rem(me + n - i, n)), :]
        return pltpu.make_async_remote_copy(
            src_ref=place, dst_ref=place, send_sem=all_send.at[i], recv_sem=all_recv.at[i],
            device_id={"wide": lax.rem(me + i, n)}, device_id_type=MESH,
        )

    for i in range(1, n):
        low_copy(i).start()
    main_piece(0, 7, True)

    def early(i, c):
        main_piece(1, i, False)
        return c

    lax.fori_loop(0, 4, early, 0)
    for i in range(1, n):
        low_copy(i).wait_recv()
    total = low_acc[own_slice(me), :]
    for i in range(1, n):
        total = total + low_parts[i]
    low_sum[own_slice(me), :] = total
    for i in range(1, n):
        all_copy(i).start()
    lax.fori_loop(4, 8, early, 0)
    acc[0] = acc[0] / (1.0 + jnp.exp(-acc[0]))
    outmap_copy.wait()
    for i in range(1, n):
        all_arrived(i).wait_recv()
    for s in range(seg_count):
        at = s * seg_size
        low = low_sum[at:at + seg_size, :rank].astype(jnp.bfloat16)
        term = jnp.dot(low, outmap[slots[s]], preferred_element_type=jnp.float32)
        value = acc[0, at:at + seg_size, :] * (
            acc[1, at:at + seg_size, :] + adapter_scale * term
        )
        position = lax.broadcasted_iota(jnp.int32, value.shape, 0)
        hidden[at:at + seg_size, :] = jnp.where(
            position < seg_length[s], value, 0.0
        ).astype(hidden.dtype)

    for i in range(1, n):
        low_copy(i).wait_send()
        all_copy(i).wait_send()

    def drain(t, carry):
        win, step = t // steps, t % steps
        for way in range(2):
            for cut in range(PARTS):
                ring_copy(way, win, cut, step).wait_send()
            pair_copy(core, way, win, step).wait_send()

            @pl.when(step == 0)
            def _():
                pair_copy(core, way, win, steps).wait_send()
        return carry

    lax.fori_loop(0, WINDOWS * steps, drain, 0)


def fused(
    tokens, gate_weight, up_weight, adapter_in, adapter_out, seg_adapter, holder_slot, seg_length
):
    n = lax.axis_size("wide")
    rows = tokens.shape[0] * n
    dim = tokens.shape[1]
    columns = gate_weight.shape[1]
    lanes = -(-adapter_in.shape[1] // 128) * 128
    chips = n // 2
    width = dim // 4 // WINDOWS
    dma = pltpu.SemaphoreType.DMA
    smem = pl.BlockSpec(memory_space=pltpu.SMEM)
    hbm = pl.BlockSpec(memory_space=pl.ANY)
    vmem = pl.BlockSpec(memory_space=pltpu.VMEM)
    return pl.pallas_call(
        functools.partial(kernel, n, seg_adapter.shape[0]),
        out_shape=jax.ShapeDtypeStruct((rows, columns), jnp.bfloat16),
        in_specs=[smem, smem, smem, vmem, hbm, hbm, hbm, hbm],
        out_specs=vmem,
        scratch_shapes=[
            pltpu.VMEM((2, 2, WINDOWS, rows, width), jnp.bfloat16),
            pltpu.VMEM((2, 4 * WINDOWS, width, columns), jnp.bfloat16),
            pltpu.VMEM((lanes, dim), jnp.bfloat16),
            pltpu.VMEM(adapter_out.shape, jnp.bfloat16),
            pltpu.VMEM((2, rows, columns), jnp.float32),
            pltpu.VMEM((rows, lanes), jnp.float32),
            pltpu.VMEM((32, dim // 2), jnp.bfloat16),
            pltpu.VMEM((32, dim // 2), jnp.bfloat16),
            pltpu.VMEM((n, rows // n, lanes), jnp.float32),
            pltpu.VMEM((rows, lanes), jnp.float32),
            dma((2, 4 * WINDOWS)),
            dma((2,)),
            dma((2,)),
            dma((2, WINDOWS, PARTS, chips - 1)),
            dma((2, WINDOWS, PARTS, chips - 1)),
            dma((2, WINDOWS, chips)),
            dma((2, WINDOWS, chips)),
            dma((n,)),
            dma((n,)),
            dma((n,)),
            dma((n,)),
        ],
        compiler_params=pltpu.CompilerParams(
            collective_id=0, has_side_effects=True, vmem_limit_bytes=60 * 1024 * 1024
        ),
        name="gated_input",
    )(seg_adapter, holder_slot, seg_length, tokens, gate_weight, up_weight, adapter_in, adapter_out)


def plain(
    tokens, gate_weight, up_weight, adapter_in, adapter_out, seg_adapter, holder_slot, seg_length
):
    holders = lax.axis_size("wide")
    my_index = lax.axis_index("wide")
    held_count = adapter_in.shape[0]
    rank_size = adapter_in.shape[1]
    model_dim = tokens.shape[1]
    row_count = tokens.shape[0] * holders
    seg_count = seg_adapter.shape[0]
    seg_size = row_count // seg_count
    columns = gate_weight.shape[1]
    pool_size = holder_slot.shape[0]
    matches = seg_adapter[:, None] == jnp.arange(pool_size, dtype=jnp.int32)[None, :]
    seg_slot = jnp.sum(jnp.where(matches, holder_slot[None, :], 0), axis=1)
    seg_owner = seg_slot // held_count
    local_slot = seg_slot % held_count
    gathered = lax.all_gather(tokens, "wide", axis=0, tiled=True)
    gate_block = jnp.dot(gathered, gate_weight, preferred_element_type=jnp.float32)
    up_weight_block = jnp.dot(gathered, up_weight, preferred_element_type=jnp.float32)

    def per_segment(operand):
        seg_rows, owner_now, slot_now = operand

        def compute():
            return lax.dot_general(
                seg_rows,
                adapter_in[slot_now],
                (((1,), (1,)), ((), ())),
                preferred_element_type=jnp.float32,
            )

        def nothing():
            return jnp.zeros((seg_size, rank_size), jnp.float32)

        return lax.cond(owner_now == my_index, compute, nothing)

    seg_blocks = gathered.reshape(seg_count, seg_size, model_dim)
    partial_in = lax.map(per_segment, (seg_blocks, seg_owner, local_slot)).reshape(
        row_count, rank_size
    )
    reduced_rank_state = lax.psum(partial_in, "wide").astype(jnp.bfloat16)
    selected_output = adapter_out[seg_slot]
    adapter_term = jnp.einsum(
        "iyg,ign->iyn",
        reduced_rank_state.reshape(seg_count, seg_size, rank_size),
        selected_output,
        preferred_element_type=jnp.float32,
    ).reshape(row_count, columns)
    up_output_total = up_weight_block + adapter_scale * adapter_term
    positions = jnp.arange(seg_size, dtype=jnp.int32)
    live_rows = (positions[None, :] < seg_length[:, None]).reshape(row_count)
    hidden = jnp.where(
        live_rows[:, None], jax.nn.silu(gate_block) * up_output_total, jnp.float32(0.0)
    )
    return hidden.astype(jnp.bfloat16)


def on_device(tokens, gate_weight, up_weight, adapter_in, *rest):
    n = lax.axis_size("wide")
    own_rows, dim = tokens.shape
    resident = 2 * (2 * dim * gate_weight.shape[1] + own_rows * n * dim)
    fits = (
        n % 4 == 0
        and gate_weight.shape[1] % 128 == 0
        and own_rows % 8 == 0
        and own_rows <= 32
        and adapter_in.shape[0] == 1
        and dim % (4 * WINDOWS * PARTS * 128) == 0
        and resident < 40 * 1024 * 1024
    )
    return (fused if fits else plain)(tokens, gate_weight, up_weight, adapter_in, *rest)


def solution(mesh):
    in_specs = (
        P(("groups", "wide"), None),
        P(None, "wide"),
        P(None, "wide"),
        P(("groups", "wide"), None, None),
        P("groups", None, "wide"),
        P("groups"),
        P("groups"),
        P("groups"),
    )
    out_specs = P("groups", "wide")
    return jax.shard_map(
        on_device, mesh=mesh, in_specs=in_specs, out_specs=out_specs, check_vma=False
    )
```
